512 devices in a mesh: pairs: 32 (over z, y_lo), rows: 16 (over x, y_hi, core).
Axes of the slice: x: 4, y: 8 (y_hi: 2, y_lo: 4; y = y_hi * 4 + y_lo), z: 8, core: 2. Of those that a mesh axis runs over, the one named last changes fastest.
Arguments:
- matrix: float32 [32768, 8192], P('rows', 'pairs'), may hold values from -9 to 9
Outputs:
- rotated: float32 [32768, 8192], P('rows', 'pairs')
- rotated_gram: float32 [8192, 256], P('pairs')
The draws below stay inside these ranges and needn't reach their ends.
All inputs are finite; a program needn't handle non-finite values.
Results may differ from the reference program's by a relative error of at most 0.0003.
Values sent between devices are 32-bit elements; how exact they have to be, the bound alone decides.
No kernel may reach another device: no remote copies, remote signals or barrier semaphores. Data moves between devices by JAX's collectives and lax.ppermute only.
A program may use at most 64 MiB of HBM per device.

```python
import jax
import jax.numpy as jnp
from jax import lax

BLK = 128
ITERS = 3
STEPS = 2
SEATS = 32
COLS = 8192
ROWS = 32768


def draw_matrix(key, part):
    key = jax.random.fold_in(key, 7)
    first_key = jax.random.fold_in(key, 0)
    second_key = jax.random.fold_in(key, 1)
    fourth_key = jax.random.fold_in(key, 3)
    column_scale = jnp.exp(jax.random.uniform(second_key, (1, COLS), jnp.float32, -0.3466, 0.3466))
    common = jnp.clip(jax.random.normal(fourth_key, (ROWS, 1), jnp.float32), -6.0, 6.0)
    values = jnp.clip(jax.random.normal(first_key, (ROWS, COLS), jnp.float32), -6.0, 6.0)
    return jnp.clip(values * column_scale + 0.2 * common, -9.0, 9.0)


def setup_inputs(seed: int = 0) -> dict:
    keys = jax.random.split(jax.random.key(seed), 2)
    matrix = draw_matrix(jax.random.fold_in(keys[1], 71), 0)
    return {"matrix": matrix}


highest = lax.Precision.HIGHEST

def right_solve(factor, values):
    return lax.linalg.triangular_solve(factor, values, left_side=False, lower=True, transpose_a=True)

def eigen_steps(gram_matrix):
    rotation = jnp.eye(gram_matrix.shape[0], dtype=jnp.float32)
    for sweep_index in range(ITERS):
        square = jnp.dot(gram_matrix.astype(jnp.float32), gram_matrix.astype(jnp.float32), precision=highest, preferred_element_type=jnp.float32)
        factor = jnp.linalg.cholesky(square)
        rotation = right_solve(factor, jnp.dot(rotation.astype(jnp.float32), gram_matrix.astype(jnp.float32), precision=highest, preferred_element_type=jnp.float32))
        gram_matrix = right_solve(factor, jnp.dot(factor.T.astype(jnp.float32), gram_matrix.astype(jnp.float32), precision=highest, preferred_element_type=jnp.float32))
        gram_matrix = 0.5 * (gram_matrix + gram_matrix.T)
    return (rotation, gram_matrix)

def reference(matrix):
    seated = matrix.reshape(ROWS, SEATS, 2, BLK)
    leading = jnp.transpose(seated[:, :, 0, :], (1, 0, 2))
    trailing = jnp.transpose(seated[:, :, 1, :], (1, 0, 2))
    for step_index in range(STEPS):
        if step_index > 0:
            new_leading = jnp.concatenate([leading[:1], trailing[:1], leading[1:SEATS - 1]], 0)
            new_trailing = jnp.concatenate([trailing[1:], leading[SEATS - 1:]], 0)
            leading, trailing = (new_leading, new_trailing)
        paired = jnp.concatenate([leading, trailing], axis=2)
        gram_matrix = jnp.einsum('srp,srq->spq', paired, paired, precision=highest) / ROWS
        rotation, gram_matrix = jax.vmap(eigen_steps)(gram_matrix)
        paired = jnp.einsum('srp,spq->srq', paired, rotation, precision=highest)
        leading, trailing = (paired[:, :, :BLK], paired[:, :, BLK:])
    rotated = jnp.transpose(paired, (1, 0, 2)).reshape(ROWS, 2 * BLK * SEATS)
    return (rotated, gram_matrix.reshape(SEATS * 2 * BLK, 2 * BLK))
```

```python
import jax
import jax.numpy as jnp
from jax import lax
from jax.experimental import pallas as pl
from jax.experimental.pallas import tpu as pltpu
from jax.sharding import PartitionSpec as P

ITERS = 3
BLK = 128
SUB = 8
TILES = BLK // SUB
WIDE = 2

highest = lax.Precision.HIGHEST


def nn(a, b):
    return lax.dot_general(
        a, b, (((1,), (0,)), ((), ())), precision=highest, preferred_element_type=jnp.float32
    )


def tn(a, b):
    return lax.dot_general(
        a, b, (((0,), (0,)), ((), ())), precision=highest, preferred_element_type=jnp.float32
    )


def nt(a, b):
    return lax.dot_general(
        a, b, (((1,), (1,)), ((), ())), precision=highest, preferred_element_type=jnp.float32
    )


def lane(x, k):
    return jnp.broadcast_to(x[:, k : k + 1], (SUB, BLK))


def row(x, k):
    return jnp.broadcast_to(x[k : k + 1, :], (SUB, BLK))


def inverse_factor(square):
    lanes = lax.broadcasted_iota(jnp.int32, (SUB, BLK), 1)
    rows = lax.broadcasted_iota(jnp.int32, (SUB, BLK), 0)
    s = [square[SUB * q : SUB * q + SUB, :] for q in range(TILES)]
    w = [None] * TILES
    for p in range(0, TILES, WIDE):
        count = SUB * WIDE
        low = SUB * p
        inside = (lanes >= low) & (lanes < low + count)
        c = [[lane(s[p + r], low + k) for r in range(WIDE)] for k in range(count)]
        a = [
            jnp.where(inside, jnp.where(lanes == rows + SUB * (p + r), 1.0, 0.0), s[p + r])
            for r in range(WIDE)
        ]
        done = [None] * WIDE
        scale = [None] * WIDE
        for k in range(count):
            t, j = divmod(k, SUB)
            pivot = row(c[k][t], j)
            inv = 1.0 / pivot
            z = row(a[t], j)
            finished = z * lax.rsqrt(pivot)
            done[t] = finished if j == 0 else jnp.where(rows == j, finished, done[t])
            scale[t] = inv if j == 0 else jnp.where(rows == j, inv, scale[t])
            column = list(c[k])
            column[t] = jnp.where(rows == j, 0.0, column[t])
            factor = [column[r] * inv for r in range(WIDE)]
            for l in range(k + 1, count):
                m = row(c[l][t], j)
                for r in range(WIDE):
                    c[l][r] = c[l][r] - factor[r] * m
            for r in range(WIDE):
                a[r] = a[r] - factor[r] * z
        for r in range(WIDE):
            w[p + r] = jnp.where(lanes <= rows + SUB * (p + r), done[r], 0.0)
        if p + WIDE < TILES:
            y = [a[r] * scale[r] for r in range(WIDE)]
            ys = [row(y[k // SUB], k % SUB) for k in range(count)]
            for q in range(p + WIDE, TILES):
                o = [lane(s[q], low + k) for k in range(count)]
                even = o[0] * ys[0]
                odd = o[1] * ys[1]
                for k in range(2, count, 2):
                    even = even + o[k] * ys[k]
                    odd = odd + o[k + 1] * ys[k + 1]
                s[q] = jnp.where(inside, 0.0, s[q]) - (even + odd)
    return jnp.concatenate(w, 0)


def eigen_kernel(lead_ref, cross_ref, trail_ref, rotation_ref, gram_ref, g, z):
    g[:BLK, :BLK] = lead_ref[...]
    g[:BLK, BLK:] = cross_ref[...]
    g[BLK:, :BLK] = cross_ref[...].T
    g[BLK:, BLK:] = trail_ref[...]
    z[...] = g[...]

    def sweep(_, carry):
        za, zc = z[:, :BLK], z[:, BLK:]
        saa = tn(za, za)
        sac = tn(za, zc)
        scc = tn(zc, zc)
        wa = inverse_factor(saa)
        t = nn(wa, sac)
        va = nt(za, wa)
        xc = zc - nn(va, t)
        wc = inverse_factor(scc - tn(t, t))
        vc = nt(xc, wc)
        rotation_ref[:, :BLK] = va
        rotation_ref[:, BLK:] = vc
        z[...] = nn(g[...], rotation_ref[...])
        return carry

    lax.fori_loop(0, ITERS, sweep, 0)
    final = tn(rotation_ref[...], z[...])
    gram_ref[...] = 0.5 * (final + final.T)


def eigen_steps(lead, cross, trail):
    full = jax.ShapeDtypeStruct((2 * BLK, 2 * BLK), jnp.float32)
    vmem = pl.BlockSpec(memory_space=pltpu.VMEM)
    return pl.pallas_call(
        eigen_kernel,
        out_shape=(full, full),
        in_specs=[vmem] * 3,
        out_specs=(vmem, vmem),
        scratch_shapes=[pltpu.VMEM((2 * BLK, 2 * BLK), jnp.float32)] * 2,
        compiler_params=pltpu.CompilerParams(vmem_limit_bytes=32 * 1024 * 1024),
        name="eigen_steps",
    )(lead, cross, trail)


def swapped(x, bit):
    return lax.ppermute(x, "rows", [(i, i ^ bit) for i in range(lax.axis_size("rows"))])


def summed_over_rows(x, halve):
    if halve:
        odd = lax.axis_index("rows") % 2 == 1
        half = x.shape[0] // 2
        keep = jnp.where(odd, x[half:], x[:half])
        give = jnp.where(odd, x[:half], x[half:])
        part = keep + swapped(give, 1)
    else:
        part = x + swapped(x, 1)
    for bit in (4, 8, 2):
        part = part + swapped(part, bit)
    if halve:
        other = swapped(part, 1)
        return jnp.where(odd, jnp.concatenate([other, part], 0), jnp.concatenate([part, other], 0))
    return part


def moved(x, distance):
    devices = range(lax.axis_size("pairs"))
    return lax.ppermute(x, "pairs", [(i - distance, i) for i in devices if i - distance in devices])


def per_device(matrix):
    seat = lax.axis_index("pairs")
    first = seat == 0
    last = seat == lax.axis_size("pairs") - 1
    rows_all = matrix.shape[0] * lax.axis_size("rows")

    local = tn(matrix, matrix)
    packed = jnp.concatenate([local[:BLK, :BLK], local[:BLK, BLK:], local[BLK:, BLK:]], 0)
    packed = summed_over_rows(packed, True) / rows_all
    rotation, gram = eigen_steps(packed[:BLK], packed[BLK : 2 * BLK], packed[2 * BLK :])

    leading = nn(matrix, rotation[:, :BLK])
    trailing = nn(matrix, rotation[:, BLK:])
    lead_gram, trail_gram = gram[:BLK, :BLK], gram[BLK:, BLK:]

    arrived = moved(jnp.where(first, trailing, leading), 1)
    from_right = moved(trailing, -1)
    arrived_gram = moved(jnp.where(first, trail_gram, lead_gram), 1)
    from_right_gram = moved(trail_gram, -1)
    new_leading = jnp.where(first, leading, arrived)
    new_trailing = jnp.where(last, leading, from_right)
    new_lead_gram = jnp.where(first, lead_gram, arrived_gram)
    new_trail_gram = jnp.where(last, lead_gram, from_right_gram)

    cross = summed_over_rows(tn(new_leading, new_trailing), False) / rows_all
    rotation, gram = eigen_steps(new_lead_gram, cross, new_trail_gram)
    paired = nn(new_leading, rotation[:BLK]) + nn(new_trailing, rotation[BLK:])
    return paired, gram


def solution(mesh):
    return jax.shard_map(
        per_device,
        mesh=mesh,
        in_specs=(P("rows", "pairs"),),
        out_specs=(P("rows", "pairs"), P("pairs", None)),
        check_vma=False,
    )
```

```python
import jax
import jax.numpy as jnp
from jax import lax
from jax.experimental import pallas as pl
from jax.experimental.pallas import tpu as pltpu
from jax.sharding import PartitionSpec as P

ITERS = 3
BLK = 128
SUB = 8
TILES = BLK // SUB
WIDE = 2
EARLY = 5

highest = lax.Precision.HIGHEST


def nn(a, b):
    return lax.dot_general(
        a, b, (((1,), (0,)), ((), ())), precision=highest, preferred_element_type=jnp.float32
    )


def tn(a, b):
    return lax.dot_general(
        a, b, (((0,), (0,)), ((), ())), precision=highest, preferred_element_type=jnp.float32
    )


def nt(a, b):
    return lax.dot_general(
        a, b, (((1,), (1,)), ((), ())), precision=highest, preferred_element_type=jnp.float32
    )


def lane(x, k):
    return jnp.broadcast_to(x[:, k : k + 1], (SUB, BLK))


def row(x, k):
    return jnp.broadcast_to(x[k : k + 1, :], (SUB, BLK))


def inverse_factor(square):
    lanes = lax.broadcasted_iota(jnp.int32, (SUB, BLK), 1)
    rows = lax.broadcasted_iota(jnp.int32, (SUB, BLK), 0)
    s = [square[SUB * q : SUB * q + SUB, :] for q in range(TILES)]
    w = [None] * TILES
    for p in range(0, TILES, WIDE):
        count = SUB * WIDE
        low = SUB * p
        inside = (lanes >= low) & (lanes < low + count)
        c = [[lane(s[p + r], low + k) for r in range(WIDE)] for k in range(count)]
        a = [
            jnp.where(inside, jnp.where(lanes == rows + SUB * (p + r), 1.0, 0.0), s[p + r])
            for r in range(WIDE)
        ]
        done = [None] * WIDE
        scale = [None] * WIDE
        for k in range(count):
            t, j = divmod(k, SUB)
            pivot = row(c[k][t], j)
            inv = 1.0 / pivot
            z = row(a[t], j)
            finished = z * lax.rsqrt(pivot)
            done[t] = finished if j == 0 else jnp.where(rows == j, finished, done[t])
            scale[t] = inv if j == 0 else jnp.where(rows == j, inv, scale[t])
            column = list(c[k])
            column[t] = jnp.where(rows == j, 0.0, column[t])
            factor = [column[r] * inv for r in range(WIDE)]
            for l in range(k + 1, count):
                m = row(c[l][t], j)
                for r in range(WIDE):
                    c[l][r] = c[l][r] - factor[r] * m
            for r in range(WIDE):
                a[r] = a[r] - factor[r] * z
        for r in range(WIDE):
            w[p + r] = jnp.where(lanes <= rows + SUB * (p + r), done[r], 0.0)
        if p + WIDE < TILES:
            y = [a[r] * scale[r] for r in range(WIDE)]
            ys = [row(y[k // SUB], k % SUB) for k in range(count)]
            for q in range(p + WIDE, TILES):
                o = [lane(s[q], low + k) for k in range(count)]
                even = o[0] * ys[0]
                odd = o[1] * ys[1]
                for k in range(2, count, 2):
                    even = even + o[k] * ys[k]
                    odd = odd + o[k + 1] * ys[k + 1]
                s[q] = jnp.where(inside, 0.0, s[q]) - (even + odd)
    return jnp.concatenate(w, 0)


def eigen_kernel(lead_ref, cross_ref, trail_ref, rotation_ref, gram_ref, g, z):
    g[:BLK, :BLK] = lead_ref[...]
    g[:BLK, BLK:] = cross_ref[...]
    g[BLK:, :BLK] = cross_ref[...].T
    g[BLK:, BLK:] = trail_ref[...]
    z[...] = g[...]

    def sweep(_, carry):
        za, zc = z[:, :BLK], z[:, BLK:]
        saa = tn(za, za)
        sac = tn(za, zc)
        scc = tn(zc, zc)
        wa = inverse_factor(saa)
        t = nn(wa, sac)
        va = nt(za, wa)
        xc = zc - nn(va, t)
        wc = inverse_factor(scc - tn(t, t))
        vc = nt(xc, wc)
        rotation_ref[:, :BLK] = va
        rotation_ref[:, BLK:] = vc
        z[...] = nn(g[...], rotation_ref[...])
        return carry

    lax.fori_loop(0, ITERS, sweep, 0)
    final = tn(rotation_ref[...], z[...])
    gram_ref[...] = 0.5 * (final + final.T)


def eigen_steps(lead, cross, trail):
    full = jax.ShapeDtypeStruct((2 * BLK, 2 * BLK), jnp.float32)
    vmem = pl.BlockSpec(memory_space=pltpu.VMEM)
    return pl.pallas_call(
        eigen_kernel,
        out_shape=(full, full),
        in_specs=[vmem] * 3,
        out_specs=(vmem, vmem),
        scratch_shapes=[pltpu.VMEM((2 * BLK, 2 * BLK), jnp.float32)] * 2,
        compiler_params=pltpu.CompilerParams(vmem_limit_bytes=32 * 1024 * 1024),
        name="eigen_steps",
    )(lead, cross, trail)


def swapped(x, bit):
    return lax.ppermute(x, "rows", [(i, i ^ bit) for i in range(lax.axis_size("rows"))])


def summed_over_x(x):
    size = lax.axis_size("rows")
    groups = [[c + (size // 4) * j for j in range(4)] for c in range(size // 4)]
    copies = jnp.broadcast_to(x[None], (4,) + x.shape)
    got = lax.all_to_all(copies, "rows", 0, 0, axis_index_groups=groups)
    return (got[0] + got[1]) + (got[2] + got[3])


def core_halves(x):
    odd = lax.axis_index("rows") % 2 == 1
    half = x.shape[0] // 2
    keep = jnp.where(odd, x[half:], x[:half])
    give = jnp.where(odd, x[:half], x[half:])
    return keep + swapped(give, 1), odd


def both_halves(part, odd):
    other = swapped(part, 1)
    return jnp.where(odd, jnp.concatenate([other, part], 0), jnp.concatenate([part, other], 0))


def moved(x, distance):
    count = lax.axis_size("pairs")
    return lax.ppermute(
        x, "pairs", [(i - distance, i) for i in range(count) if 0 <= i - distance < count]
    )


def big(a, b, dims):
    return lax.dot_general(
        a, b, (dims, ((), ())), precision=lax.Precision.HIGH, preferred_element_type=jnp.float32
    )


def per_device(matrix):
    seat = lax.axis_index("pairs")
    first = seat == 0
    last = seat == lax.axis_size("pairs") - 1
    rows_all = matrix.shape[0] * lax.axis_size("rows")
    early = matrix.shape[0] * EARLY // 16

    local = big(matrix, matrix, ((0,), (0,)))
    packed = jnp.concatenate([local[:BLK, :BLK], local[:BLK, BLK:], local[BLK:, BLK:]], 0)
    part, odd = core_halves(packed)
    part = part + swapped(part, 2)

    part, columns = lax.optimization_barrier((part, matrix[:early]))
    from_left = moved(columns, 1)
    from_right = moved(columns, -1)

    packed = both_halves(summed_over_x(part), odd) / rows_all
    rotation, gram = eigen_steps(packed[:BLK], packed[BLK : 2 * BLK], packed[2 * BLK :])

    rotation, gram, from_left, from_right = lax.optimization_barrier(
        (rotation, gram, from_left, from_right)
    )
    to_lead, to_trail = rotation[:, :BLK], rotation[:, BLK:]
    lead_gram, trail_gram = gram[:BLK, :BLK], gram[BLK:, BLK:]
    ahead = jnp.where(first, to_trail, to_lead)
    ahead_gram = jnp.where(first, trail_gram, lead_gram)
    rest = matrix[early:]
    over_left = moved(jnp.concatenate([ahead, ahead_gram, big(rest, ahead, ((1,), (0,)))], 0), 1)
    over_right = moved(
        jnp.concatenate([to_trail, trail_gram, big(rest, to_trail, ((1,), (0,)))], 0), -1
    )
    own = big(matrix, to_lead, ((1,), (0,)))
    turned_left = big(from_left, over_left[: 2 * BLK], ((1,), (0,)))
    turned_right = big(from_right, over_right[: 2 * BLK], ((1,), (0,)))
    new_leading = jnp.where(first, own, jnp.concatenate([turned_left, over_left[3 * BLK :]], 0))
    new_trailing = jnp.where(last, own, jnp.concatenate([turned_right, over_right[3 * BLK :]], 0))
    new_lead_gram = jnp.where(first, lead_gram, over_left[2 * BLK : 3 * BLK])
    new_trail_gram = jnp.where(last, lead_gram, over_right[2 * BLK : 3 * BLK])

    cross = big(new_leading, new_trailing, ((0,), (0,)))
    cross = cross + swapped(cross, 1)
    cross = summed_over_x(cross)
    cross = (cross + swapped(cross, 2)) / rows_all
    rotation, gram = eigen_steps(new_lead_gram, cross, new_trail_gram)
    paired = big(new_leading, rotation[:BLK], ((1,), (0,)))
    paired = paired + big(new_trailing, rotation[BLK:], ((1,), (0,)))
    return paired, gram


def solution(mesh):
    return jax.shard_map(
        per_device,
        mesh=mesh,
        in_specs=(P("rows", "pairs"),),
        out_specs=(P("rows", "pairs"), P("pairs", None)),
        check_vma=False,
    )
```

```python
import jax
import jax.numpy as jnp
from jax import lax
from jax.experimental import pallas as pl
from jax.experimental.pallas import tpu as pltpu
from jax.sharding import PartitionSpec as P

ITERS = 3
BLK = 128
SUB = 8
LANES = 128
PANEL = 64
WIDE = 2
SQUARE = 2
TURN = 3
AHEAD = 2
EARLY = 5

highest = lax.Precision.HIGHEST


def nn(a, b):
    return lax.dot_general(
        a, b, (((1,), (0,)), ((), ())), precision=highest, preferred_element_type=jnp.float32
    )


def tn(a, b):
    return lax.dot_general(
        a, b, (((0,), (0,)), ((), ())), precision=highest, preferred_element_type=jnp.float32
    )


def nt(a, b):
    return lax.dot_general(
        a, b, (((1,), (1,)), ((), ())), precision=highest, preferred_element_type=jnp.float32
    )


def lane(x, k):
    return jnp.broadcast_to(x[:, k : k + 1], (SUB, LANES))


def row(x, k):
    return jnp.broadcast_to(x[k : k + 1, :], (SUB, LANES))


def inverse_factors(squares, wide, beside):
    lanes = lax.broadcasted_iota(jnp.int32, (SUB, LANES), 1)
    rows = lax.broadcasted_iota(jnp.int32, (SUB, LANES), 0)
    blank = jnp.zeros((SUB, LANES - PANEL), jnp.float32)
    tiles = PANEL // SUB
    tables = [
        [jnp.concatenate([s[SUB * q : SUB * q + SUB, :], blank], 1) for q in range(tiles)]
        for s in squares
    ]
    factors = [[None] * tiles for _ in squares]
    count = SUB * wide
    for p in range(0, tiles, wide):
        low = SUB * p
        inside = (lanes >= low) & (lanes < low + count)
        states = []
        for s in tables:
            c = [[lane(s[p + r], low + k) for r in range(wide)] for k in range(count)]
            a = [
                jnp.where(inside, jnp.where(lanes == rows + SUB * (p + r), 1.0, 0.0), s[p + r])
                for r in range(wide)
            ]
            states.append((c, a, [None] * wide, [None] * wide))
        for k in range(count):
            next(beside, None)
            t, j = divmod(k, SUB)
            for c, a, done, scale in states:
                pivot = row(c[k][t], j)
                inv = 1.0 / pivot
                z = row(a[t], j)
                finished = z * lax.rsqrt(pivot)
                done[t] = finished if j == 0 else jnp.where(rows == j, finished, done[t])
                scale[t] = inv if j == 0 else jnp.where(rows == j, inv, scale[t])
                column = list(c[k])
                column[t] = jnp.where(rows == j, 0.0, column[t])
                factor = [column[r] * inv for r in range(wide)]
                for l in range(k + 1, count):
                    m = row(c[l][t], j)
                    for r in range(wide):
                        c[l][r] = c[l][r] - factor[r] * m
                for r in range(wide):
                    a[r] = a[r] - factor[r] * z
        for s, w, (c, a, done, scale) in zip(tables, factors, states):
            for r in range(wide):
                w[p + r] = jnp.where(lanes <= rows + SUB * (p + r), done[r], 0.0)
            if p + wide < tiles:
                y = [a[r] * scale[r] for r in range(wide)]
                ys = [row(y[k // SUB], k % SUB) for k in range(count)]
                for q in range(p + wide, tiles):
                    o = [lane(s[q], low + k) for k in range(count)]
                    even = o[0] * ys[0]
                    odd = o[1] * ys[1]
                    for k in range(2, count, 2):
                        even = even + o[k] * ys[k]
                        odd = odd + o[k + 1] * ys[k + 1]
                    s[q] = jnp.where(inside, 0.0, s[q]) - (even + odd)
    for _ in beside:
        pass
    return [jnp.concatenate(w, 0)[:, :PANEL] for w in factors]


def parts(x, count):
    found = []
    for _ in range(count - 1):
        head = x.astype(jnp.bfloat16)
        found.append(head)
        x = x - head.astype(jnp.float32)
    return found + [x.astype(jnp.bfloat16)]


def product_steps(a, b, dims):
    count = min(len(a), len(b))
    total = None
    for order in reversed(range(count)):
        for i in range(order + 1):
            term = lax.dot_general(
                a[i], b[order - i], (dims, ((), ())), preferred_element_type=jnp.float32
            )
            total = term if total is None else total + term
            yield
    return total


def product(a, b, dims):
    steps = product_steps(a, b, dims)
    while True:
        try:
            next(steps)
        except StopIteration as end:
            return end.value


def ahead_steps(states, known, fixed, found):
    for t, x, along in states:
        if along is not None:
            x = x - (yield from product_steps(along, known[t], NN))
        far = yield from product_steps(parts(x, AHEAD), fixed, NN)
        found.append(parts(jnp.concatenate([x, far], 1), TURN))


NN = ((1,), (0,))
NT = ((1,), (1,))


def eigen_kernel(lead_ref, cross_ref, trail_ref, rotation_ref, gram_ref, g, turns, z):
    cross = cross_ref[...]
    g[:BLK, :BLK] = lead_ref[...]
    g[:BLK, BLK:] = cross
    g[BLK:, :BLK] = cross.T
    g[BLK:, BLK:] = trail_ref[...]
    panels = 2 * BLK // PANEL
    fixed = parts(g[...], AHEAD)
    ready = {(0, j): g[PANEL * j : PANEL * j + PANEL, :] for j in range(panels)}
    known = {t: None for t in range(ITERS)}
    for stage in range(panels + ITERS - 1):
        active = [(t, stage - t) for t in range(ITERS) if 0 <= stage - t < panels]
        squares, states = [], []
        for t, j in active:
            x = ready.pop((t, j))
            split = parts(x, SQUARE)
            square = product(split, split, NT)
            along = None
            if j > 0:
                along = parts(product(split, known[t], NT), SQUARE)
                square = square - product(along, along, NT)
            squares.append(square)
            states.append((t, x, along))
        found = []
        factors = inverse_factors(squares, WIDE, ahead_steps(states, known, fixed, found))
        for (t, j), both, w in zip(active, found, factors):
            both = product(parts(w, TURN), both, NN)
            turn, ahead = both[:, : 2 * BLK], both[:, 2 * BLK :]
            turns[t, PANEL * j : PANEL * j + PANEL, :] = turn
            if j + 1 < panels:
                split = parts(turn, SQUARE)
                old = known[t]
                known[t] = split if old is None else [
                    jnp.concatenate([a, b], 0) for a, b in zip(old, split)
                ]
            if t + 1 < ITERS:
                ready[t + 1, j] = ahead
            else:
                z[PANEL * j : PANEL * j + PANEL, :] = ahead
    turned = turns[ITERS - 1]
    final = product(parts(turned, AHEAD), parts(z[...], AHEAD), NT)
    rotation_ref[...] = turned.T
    gram_ref[...] = 0.5 * (final + final.T)


def eigen_steps(lead, cross, trail):
    full = jax.ShapeDtypeStruct((2 * BLK, 2 * BLK), jnp.float32)
    vmem = pl.BlockSpec(memory_space=pltpu.VMEM)
    return pl.pallas_call(
        eigen_kernel,
        out_shape=(full, full),
        in_specs=[vmem] * 3,
        out_specs=(vmem, vmem),
        scratch_shapes=[
            pltpu.VMEM((2 * BLK, 2 * BLK), jnp.float32),
            pltpu.VMEM((ITERS, 2 * BLK, 2 * BLK), jnp.float32),
            pltpu.VMEM((2 * BLK, 2 * BLK), jnp.float32),
        ],
        compiler_params=pltpu.CompilerParams(vmem_limit_bytes=32 * 1024 * 1024),
        name="eigen_steps",
    )(lead, cross, trail)


def swapped(x, bit):
    return lax.ppermute(x, "rows", [(i, i ^ bit) for i in range(lax.axis_size("rows"))])


def summed_over_x(x):
    size = lax.axis_size("rows")
    groups = [[c + (size // 4) * j for j in range(4)] for c in range(size // 4)]
    copies = jnp.broadcast_to(x[None], (4,) + x.shape)
    got = lax.all_to_all(copies, "rows", 0, 0, axis_index_groups=groups)
    return (got[0] + got[1]) + (got[2] + got[3])


def core_halves(x):
    odd = lax.axis_index("rows") % 2 == 1
    half = x.shape[0] // 2
    keep = jnp.where(odd, x[half:], x[:half])
    give = jnp.where(odd, x[:half], x[half:])
    return keep + swapped(give, 1), odd


def both_halves(part, odd):
    other = swapped(part, 1)
    return jnp.where(odd, jnp.concatenate([other, part], 0), jnp.concatenate([part, other], 0))


def moved(x, distance):
    count = lax.axis_size("pairs")
    return lax.ppermute(
        x, "pairs", [(i - distance, i) for i in range(count) if 0 <= i - distance < count]
    )


def big(a, b, dims):
    return lax.dot_general(
        a, b, (dims, ((), ())), precision=lax.Precision.HIGH, preferred_element_type=jnp.float32
    )


def per_device(matrix):
    seat = lax.axis_index("pairs")
    first = seat == 0
    last = seat == lax.axis_size("pairs") - 1
    rows_all = matrix.shape[0] * lax.axis_size("rows")
    early = matrix.shape[0] * EARLY // 16

    local = big(matrix, matrix, ((0,), (0,)))
    packed = jnp.concatenate([local[:BLK, :BLK], local[:BLK, BLK:], local[BLK:, BLK:]], 0)
    part, odd = core_halves(packed)
    part = part + swapped(part, 2)

    part, columns = lax.optimization_barrier((part, matrix[:early]))
    from_left = moved(columns, 1)
    from_right = moved(columns, -1)

    packed = both_halves(summed_over_x(part), odd) / rows_all
    rotation, gram = eigen_steps(packed[:BLK], packed[BLK : 2 * BLK], packed[2 * BLK :])

    rotation, gram, from_left, from_right = lax.optimization_barrier(
        (rotation, gram, from_left, from_right)
    )
    to_lead, to_trail = rotation[:, :BLK], rotation[:, BLK:]
    lead_gram, trail_gram = gram[:BLK, :BLK], gram[BLK:, BLK:]
    ahead = jnp.where(first, to_trail, to_lead)
    ahead_gram = jnp.where(first, trail_gram, lead_gram)
    rest = matrix[early:]
    over_left = moved(jnp.concatenate([ahead, ahead_gram, big(rest, ahead, ((1,), (0,)))], 0), 1)
    over_right = moved(
        jnp.concatenate([to_trail, trail_gram, big(rest, to_trail, ((1,), (0,)))], 0), -1
    )
    own = big(matrix, to_lead, ((1,), (0,)))
    turned_left = big(from_left, over_left[: 2 * BLK], ((1,), (0,)))
    turned_right = big(from_right, over_right[: 2 * BLK], ((1,), (0,)))
    new_leading = jnp.where(first, own, jnp.concatenate([turned_left, over_left[3 * BLK :]], 0))
    new_trailing = jnp.where(last, own, jnp.concatenate([turned_right, over_right[3 * BLK :]], 0))
    new_lead_gram = jnp.where(first, lead_gram, over_left[2 * BLK : 3 * BLK])
    new_trail_gram = jnp.where(last, lead_gram, over_right[2 * BLK : 3 * BLK])

    cross = big(new_leading, new_trailing, ((0,), (0,)))
    cross = cross + swapped(cross, 1)
    cross = summed_over_x(cross)
    cross = (cross + swapped(cross, 2)) / rows_all
    rotation, gram = eigen_steps(new_lead_gram, cross, new_trail_gram)
    paired = big(new_leading, rotation[:BLK], ((1,), (0,)))
    paired = paired + big(new_trailing, rotation[BLK:], ((1,), (0,)))
    return paired, gram


def solution(mesh):
    return jax.shard_map(
        per_device,
        mesh=mesh,
        in_specs=(P("rows", "pairs"),),
        out_specs=(P("rows", "pairs"), P("pairs", None)),
        check_vma=False,
    )
```

```python
import jax
import jax.numpy as jnp
from jax import lax
from jax.experimental import pallas as pl
from jax.experimental.pallas import tpu as pltpu
from jax.sharding import PartitionSpec as P

ITERS = 3
BLK = 128
SUB = 8
LANES = 128
PANEL = 64
WIDE = 2
SQUARE = 2
TURN = 3
AHEAD = 2
WHOLE = 58 * 1024 * 1024
STEP = 512
EARLY = 4

highest = lax.Precision.HIGHEST


def nn(a, b):
    return lax.dot_general(
        a, b, (((1,), (0,)), ((), ())), precision=highest, preferred_element_type=jnp.float32
    )


def tn(a, b):
    return lax.dot_general(
        a, b, (((0,), (0,)), ((), ())), precision=highest, preferred_element_type=jnp.float32
    )


def nt(a, b):
    return lax.dot_general(
        a, b, (((1,), (1,)), ((), ())), precision=highest, preferred_element_type=jnp.float32
    )


def lane(x, k):
    return jnp.broadcast_to(x[:, k : k + 1], (SUB, LANES))


def row(x, k):
    return jnp.broadcast_to(x[k : k + 1, :], (SUB, LANES))


def inverse_factors(squares, wide, beside):
    lanes = lax.broadcasted_iota(jnp.int32, (SUB, LANES), 1)
    rows = lax.broadcasted_iota(jnp.int32, (SUB, LANES), 0)
    blank = jnp.zeros((SUB, LANES - PANEL), jnp.float32)
    tiles = PANEL // SUB
    tables = [
        [jnp.concatenate([s[SUB * q : SUB * q + SUB, :], blank], 1) for q in range(tiles)]
        for s in squares
    ]
    factors = [[None] * tiles for _ in squares]
    count = SUB * wide
    for p in range(0, tiles, wide):
        low = SUB * p
        inside = (lanes >= low) & (lanes < low + count)
        states = []
        for s in tables:
            c = [[lane(s[p + r], low + k) for r in range(wide)] for k in range(count)]
            a = [
                jnp.where(inside, jnp.where(lanes == rows + SUB * (p + r), 1.0, 0.0), s[p + r])
                for r in range(wide)
            ]
            states.append((c, a, [None] * wide, [None] * wide))
        for k in range(count):
            next(beside, None)
            t, j = divmod(k, SUB)
            for c, a, done, scale in states:
                pivot = row(c[k][t], j)
                inv = 1.0 / pivot
                z = row(a[t], j)
                finished = z * lax.rsqrt(pivot)
                done[t] = finished if j == 0 else jnp.where(rows == j, finished, done[t])
                scale[t] = inv if j == 0 else jnp.where(rows == j, inv, scale[t])
                column = list(c[k])
                column[t] = jnp.where(rows == j, 0.0, column[t])
                factor = [column[r] * inv for r in range(wide)]
                for l in range(k + 1, count):
                    m = row(c[l][t], j)
                    for r in range(wide):
                        c[l][r] = c[l][r] - factor[r] * m
                for r in range(wide):
                    a[r] = a[r] - factor[r] * z
        for s, w, (c, a, done, scale) in zip(tables, factors, states):
            for r in range(wide):
                w[p + r] = jnp.where(lanes <= rows + SUB * (p + r), done[r], 0.0)
            if p + wide < tiles:
                y = [a[r] * scale[r] for r in range(wide)]
                ys = [row(y[k // SUB], k % SUB) for k in range(count)]
                for q in range(p + wide, tiles):
                    o = [lane(s[q], low + k) for k in range(count)]
                    even = o[0] * ys[0]
                    odd = o[1] * ys[1]
                    for k in range(2, count, 2):
                        even = even + o[k] * ys[k]
                        odd = odd + o[k + 1] * ys[k + 1]
                    s[q] = jnp.where(inside, 0.0, s[q]) - (even + odd)
    for _ in beside:
        pass
    return [jnp.concatenate(w, 0)[:, :PANEL] for w in factors]


def parts(x, count):
    found = []
    for _ in range(count - 1):
        head = x.astype(jnp.bfloat16)
        found.append(head)
        x = x - head.astype(jnp.float32)
    return found + [x.astype(jnp.bfloat16)]


def product_steps(a, b, dims):
    count = min(len(a), len(b))
    total = None
    for order in reversed(range(count)):
        for i in range(order + 1):
            term = lax.dot_general(
                a[i], b[order - i], (dims, ((), ())), preferred_element_type=jnp.float32
            )
            total = term if total is None else total + term
            yield
    return total


def product(a, b, dims):
    steps = product_steps(a, b, dims)
    while True:
        try:
            next(steps)
        except StopIteration as end:
            return end.value


def ahead_steps(states, known, fixed, found):
    for t, x, along in states:
        if along is not None:
            x = x - (yield from product_steps(along, known[t], NN))
        far = yield from product_steps(parts(x, AHEAD), fixed, NN)
        found.append(parts(jnp.concatenate([x, far], 1), TURN))


NN = ((1,), (0,))
NT = ((1,), (1,))
TN = ((0,), (0,))


def eigen_kernel(lead_ref, cross_ref, trail_ref, rotation_ref, gram_ref, g, turns, z):
    cross = cross_ref[...]
    g[:BLK, :BLK] = lead_ref[...]
    g[:BLK, BLK:] = cross
    g[BLK:, :BLK] = cross.T
    g[BLK:, BLK:] = trail_ref[...]
    panels = 2 * BLK // PANEL
    fixed = parts(g[...], AHEAD)
    ready = {(0, j): g[PANEL * j : PANEL * j + PANEL, :] for j in range(panels)}
    known = {t: None for t in range(ITERS)}
    for stage in range(panels + ITERS - 1):
        active = [(t, stage - t) for t in range(ITERS) if 0 <= stage - t < panels]
        squares, states = [], []
        for t, j in active:
            x = ready.pop((t, j))
            split = parts(x, SQUARE)
            square = product(split, split, NT)
            along = None
            if j > 0:
                along = parts(product(split, known[t], NT), SQUARE)
                square = square - product(along, along, NT)
            squares.append(square)
            states.append((t, x, along))
        found = []
        factors = inverse_factors(squares, WIDE, ahead_steps(states, known, fixed, found))
        for (t, j), both, w in zip(active, found, factors):
            both = product(parts(w, TURN), both, NN)
            turn, ahead = both[:, : 2 * BLK], both[:, 2 * BLK :]
            turns[t, PANEL * j : PANEL * j + PANEL, :] = turn
            if j + 1 < panels:
                split = parts(turn, SQUARE)
                old = known[t]
                known[t] = split if old is None else [
                    jnp.concatenate([a, b], 0) for a, b in zip(old, split)
                ]
            if t + 1 < ITERS:
                ready[t + 1, j] = ahead
            else:
                z[PANEL * j : PANEL * j + PANEL, :] = ahead
    turned = turns[ITERS - 1]
    final = product(parts(turned, AHEAD), parts(z[...], AHEAD), NT)
    rotation_ref[...] = turned.T
    gram_ref[...] = 0.5 * (final + final.T)


def eigen_steps(lead, cross, trail):
    full = jax.ShapeDtypeStruct((2 * BLK, 2 * BLK), jnp.float32)
    vmem = pl.BlockSpec(memory_space=pltpu.VMEM)
    return pl.pallas_call(
        eigen_kernel,
        out_shape=(full, full),
        in_specs=[vmem] * 3,
        out_specs=(vmem, vmem),
        scratch_shapes=[
            pltpu.VMEM((2 * BLK, 2 * BLK), jnp.float32),
            pltpu.VMEM((ITERS, 2 * BLK, 2 * BLK), jnp.float32),
            pltpu.VMEM((2 * BLK, 2 * BLK), jnp.float32),
        ],
        compiler_params=pltpu.CompilerParams(vmem_limit_bytes=32 * 1024 * 1024),
        name="eigen_steps",
    )(lead, cross, trail)


def swapped(x, bit):
    return lax.ppermute(x, "rows", [(i, i ^ bit) for i in range(lax.axis_size("rows"))])


def summed_over(x, groups):
    copies = jnp.broadcast_to(x[None], (len(groups[0]),) + x.shape)
    got = lax.all_to_all(copies, "rows", 0, 0, axis_index_groups=groups)
    return jnp.sum(got, 0)


def along_x():
    size = lax.axis_size("rows")
    return [[c + (size // 4) * j for j in range(4)] for c in range(size // 4)]


def core_halves(x):
    odd = lax.axis_index("rows") % 2 == 1
    half = x.shape[0] // 2
    keep = jnp.where(odd, x[half:], x[:half])
    give = jnp.where(odd, x[:half], x[half:])
    return keep + swapped(give, 1), odd


def both_halves(part, odd):
    other = swapped(part, 1)
    return jnp.where(odd, jnp.concatenate([other, part], 0), jnp.concatenate([part, other], 0))


def moved(x, distance):
    count = lax.axis_size("pairs")
    return lax.ppermute(
        x, "pairs", [(i - distance, i) for i in range(count) if 0 <= i - distance < count]
    )


def big(a, b, dims):
    return lax.dot_general(
        a, b, (dims, ((), ())), precision=lax.Precision.HIGH, preferred_element_type=jnp.float32
    )


def gram_kernel(columns_ref, gram_ref):
    @pl.when(pl.program_id(0) == 0)
    def _():
        gram_ref[...] = jnp.zeros_like(gram_ref)

    split = parts(columns_ref[...], 2)
    gram_ref[...] += product(split, split, TN)


def local_gram(columns):
    rows, width = columns.shape
    return pl.pallas_call(
        gram_kernel,
        grid=(rows // STEP,),
        out_shape=jax.ShapeDtypeStruct((width, width), jnp.float32),
        in_specs=[pl.BlockSpec((STEP, width), lambda i: (i, 0))],
        out_specs=pl.BlockSpec((width, width), lambda i: (0, 0)),
        compiler_params=pltpu.CompilerParams(vmem_limit_bytes=WHOLE),
        name="local_gram",
    )(columns)


def send_kernel(ends_ref, columns_ref, rotation_ref, gram_ref, ahead_ref, back_ref):
    step = pl.program_id(0)
    steps = pl.num_programs(0)
    first = ends_ref[0] == 1
    to_lead, to_trail = rotation_ref[:, :BLK], rotation_ref[:, BLK:]
    ahead = jnp.where(first, to_trail, to_lead)

    @pl.when(step < steps - 1)
    def _():
        both = parts(jnp.concatenate([ahead, to_trail], 1), 2)
        turned = product(parts(columns_ref[...], 2), both, NN)
        ahead_ref[...] = turned[:, :BLK]
        back_ref[...] = turned[:, BLK:]

    @pl.when(step == steps - 1)
    def _():
        trail_gram = gram_ref[BLK:, BLK:]
        ahead_ref[: 2 * BLK, :] = ahead
        ahead_ref[2 * BLK :, :] = jnp.where(first, trail_gram, gram_ref[:BLK, :BLK])
        back_ref[: 2 * BLK, :] = to_trail
        back_ref[2 * BLK :, :] = trail_gram


def to_send(ends, matrix, rotation, gram, late):
    step = 3 * BLK
    steps = late // step
    payload = jax.ShapeDtypeStruct((late + step, BLK), jnp.float32)
    block = pl.BlockSpec((step, BLK), lambda i: (i, 0))
    whole = pl.BlockSpec((2 * BLK, 2 * BLK), lambda i: (0, 0))
    return pl.pallas_call(
        send_kernel,
        grid=(steps + 1,),
        out_shape=(payload, payload),
        in_specs=[
            pl.BlockSpec(memory_space=pltpu.SMEM),
            pl.BlockSpec((step, 2 * BLK), lambda i: (jnp.minimum(i, steps - 1), 0)),
            whole,
            whole,
        ],
        out_specs=(block, block),
        compiler_params=pltpu.CompilerParams(vmem_limit_bytes=32 * 1024 * 1024),
        name="to_send",
    )(ends, matrix, rotation, gram)


def arrive_kernel(
    ends_ref, own_ref, left_ref, left_turn_ref, from_left_ref, right_ref, right_turn_ref,
    from_right_ref, paired_ref, cross_ref,
):
    step = pl.program_id(0)
    steps = pl.num_programs(0)

    @pl.when(step == 0)
    def _():
        cross_ref[...] = jnp.zeros_like(cross_ref)

    def place(left, right):
        leading = jnp.where(ends_ref[0] == 1, own_ref[...], left)
        trailing = jnp.where(ends_ref[1] == 1, own_ref[...], right)
        paired_ref[:, :BLK] = leading
        paired_ref[:, BLK:] = trailing
        cross_ref[...] += product(parts(leading, 2), parts(trailing, 2), TN)

    @pl.when(step < steps - 1)
    def _():
        place(left_ref[...], right_ref[...])

    @pl.when(step == steps - 1)
    def _():
        place(
            product(parts(from_left_ref[...], 2), parts(left_turn_ref[...], 2), NN),
            product(parts(from_right_ref[...], 2), parts(right_turn_ref[...], 2), NN),
        )


def arrived_pair(ends, own, over_left, from_left, over_right, from_right):
    rows = own.shape[0]
    early = from_left.shape[0]
    steps = rows // early
    turn_at = (rows - early) // (2 * BLK)
    over = pl.BlockSpec((early, BLK), lambda i: (jnp.minimum(i, steps - 2), 0))
    turn = pl.BlockSpec((2 * BLK, BLK), lambda i: (turn_at, 0))
    moved_columns = pl.BlockSpec((early, 2 * BLK), lambda i: (0, 0))
    return pl.pallas_call(
        arrive_kernel,
        grid=(steps,),
        out_shape=(
            jax.ShapeDtypeStruct((rows, 2 * BLK), jnp.float32),
            jax.ShapeDtypeStruct((BLK, BLK), jnp.float32),
        ),
        in_specs=[
            pl.BlockSpec(memory_space=pltpu.SMEM),
            pl.BlockSpec((early, BLK), lambda i: (i, 0)),
            over, turn, moved_columns, over, turn, moved_columns,
        ],
        out_specs=(
            pl.BlockSpec((early, 2 * BLK), lambda i: (i, 0)),
            pl.BlockSpec((BLK, BLK), lambda i: (0, 0)),
        ),
        compiler_params=pltpu.CompilerParams(vmem_limit_bytes=32 * 1024 * 1024),
        name="arrived_pair",
    )(ends, own, over_left, over_left, from_left, over_right, over_right, from_right)


def turn_kernel(columns_ref, rotation_ref, paired_ref):
    rotation = parts(rotation_ref[...], 2)
    paired_ref[...] = product(parts(columns_ref[...], 2), rotation, NN)


def turned_pair(columns, rotation):
    rows, width = columns.shape
    block = pl.BlockSpec((STEP, width), lambda i: (i, 0))
    return pl.pallas_call(
        turn_kernel,
        grid=(rows // STEP,),
        out_shape=jax.ShapeDtypeStruct((rows, width), jnp.float32),
        in_specs=[block, pl.BlockSpec((width, width), lambda i: (0, 0))],
        out_specs=block,
        compiler_params=pltpu.CompilerParams(vmem_limit_bytes=WHOLE),
        name="turned_pair",
    )(columns, rotation)


def per_device(matrix):
    seat = lax.axis_index("pairs")
    first = seat == 0
    last = seat == lax.axis_size("pairs") - 1
    ends = jnp.stack([first, last]).astype(jnp.int32)
    rows_all = matrix.shape[0] * lax.axis_size("rows")
    late = matrix.shape[0] - matrix.shape[0] // EARLY

    local = local_gram(matrix)
    packed = jnp.concatenate([local[:BLK, :BLK], local[:BLK, BLK:], local[BLK:, BLK:]], 0)
    part, odd = core_halves(packed)
    part = part + swapped(part, 2)

    part, columns = lax.optimization_barrier((part, matrix[late:]))
    from_left = moved(columns, 1)
    from_right = moved(columns, -1)

    packed = both_halves(summed_over(part, along_x()), odd) / rows_all
    rotation, gram = eigen_steps(packed[:BLK], packed[BLK : 2 * BLK], packed[2 * BLK :])
    rotation, gram, from_left, from_right = lax.optimization_barrier(
        (rotation, gram, from_left, from_right)
    )

    ahead, back = to_send(ends, matrix, rotation, gram, late)
    over_left = moved(ahead, 1)
    over_right = moved(back, -1)
    own = big(matrix, rotation[:, :BLK], ((1,), (0,)))
    columns, cross = arrived_pair(ends, own, over_left, from_left, over_right, from_right)
    lead_gram = gram[:BLK, :BLK]
    at = late + 2 * BLK
    new_lead_gram = jnp.where(first, lead_gram, over_left[at:])
    new_trail_gram = jnp.where(last, lead_gram, over_right[at:])

    cross = summed_over(cross + swapped(cross, 1), along_x())
    cross = (cross + swapped(cross, 2)) / rows_all
    rotation, gram = eigen_steps(new_lead_gram, cross, new_trail_gram)
    return turned_pair(columns, rotation), gram


def solution(mesh):
    return jax.shard_map(
        per_device,
        mesh=mesh,
        in_specs=(P("rows", "pairs"),),
        out_specs=(P("rows", "pairs"), P("pairs", None)),
        check_vma=False,
    )
```

```python
import jax
import jax.numpy as jnp
from jax import lax
from jax.experimental import pallas as pl
from jax.experimental.pallas import tpu as pltpu
from jax.sharding import PartitionSpec as P

ITERS = 3
BLK = 128
SUB = 8
LANES = 128
PANEL = 64
WIDE = 2
SQUARE = 2
TURN = 3
AHEAD = 2
STEP = 512
EARLY = 4

highest = lax.Precision.HIGHEST


def nn(a, b):
    return lax.dot_general(
        a, b, (((1,), (0,)), ((), ())), precision=highest, preferred_element_type=jnp.float32
    )


def tn(a, b):
    return lax.dot_general(
        a, b, (((0,), (0,)), ((), ())), precision=highest, preferred_element_type=jnp.float32
    )


def nt(a, b):
    return lax.dot_general(
        a, b, (((1,), (1,)), ((), ())), precision=highest, preferred_element_type=jnp.float32
    )


def lane(x, k):
    return jnp.broadcast_to(x[:, k : k + 1], (SUB, LANES))


def row(x, k):
    return jnp.broadcast_to(x[k : k + 1, :], (SUB, LANES))


def inverse_factors(squares, wide, beside):
    lanes = lax.broadcasted_iota(jnp.int32, (SUB, LANES), 1)
    rows = lax.broadcasted_iota(jnp.int32, (SUB, LANES), 0)
    blank = jnp.zeros((SUB, LANES - PANEL), jnp.float32)
    tiles = PANEL // SUB
    tables = [
        [jnp.concatenate([s[SUB * q : SUB * q + SUB, :], blank], 1) for q in range(tiles)]
        for s in squares
    ]
    factors = [[None] * tiles for _ in squares]
    count = SUB * wide
    for p in range(0, tiles, wide):
        low = SUB * p
        inside = (lanes >= low) & (lanes < low + count)
        states = []
        for s in tables:
            c = [[lane(s[p + r], low + k) for r in range(wide)] for k in range(count)]
            a = [
                jnp.where(inside, jnp.where(lanes == rows + SUB * (p + r), 1.0, 0.0), s[p + r])
                for r in range(wide)
            ]
            states.append((c, a, [None] * wide, [None] * wide))
        for k in range(count):
            next(beside, None)
            t, j = divmod(k, SUB)
            for c, a, done, scale in states:
                pivot = row(c[k][t], j)
                inv = 1.0 / pivot
                z = row(a[t], j)
                finished = z * lax.rsqrt(pivot)
                done[t] = finished if j == 0 else jnp.where(rows == j, finished, done[t])
                scale[t] = inv if j == 0 else jnp.where(rows == j, inv, scale[t])
                column = list(c[k])
                column[t] = jnp.where(rows == j, 0.0, column[t])
                factor = [column[r] * inv for r in range(wide)]
                for l in range(k + 1, count):
                    m = row(c[l][t], j)
                    for r in range(wide):
                        c[l][r] = c[l][r] - factor[r] * m
                for r in range(wide):
                    a[r] = a[r] - factor[r] * z
        for s, w, (c, a, done, scale) in zip(tables, factors, states):
            for r in range(wide):
                w[p + r] = jnp.where(lanes <= rows + SUB * (p + r), done[r], 0.0)
            if p + wide < tiles:
                y = [a[r] * scale[r] for r in range(wide)]
                ys = [row(y[k // SUB], k % SUB) for k in range(count)]
                for q in range(p + wide, tiles):
                    o = [lane(s[q], low + k) for k in range(count)]
                    even = o[0] * ys[0]
                    odd = o[1] * ys[1]
                    for k in range(2, count, 2):
                        even = even + o[k] * ys[k]
                        odd = odd + o[k + 1] * ys[k + 1]
                    s[q] = jnp.where(inside, 0.0, s[q]) - (even + odd)
    for _ in beside:
        pass
    return [jnp.concatenate(w, 0)[:, :PANEL] for w in factors]


def parts(x, count):
    found = []
    for _ in range(count - 1):
        head = x.astype(jnp.bfloat16)
        found.append(head)
        x = x - head.astype(jnp.float32)
    return found + [x.astype(jnp.bfloat16)]


def product_steps(a, b, dims):
    count = min(len(a), len(b))
    total = None
    for order in reversed(range(count)):
        for i in range(order + 1):
            term = lax.dot_general(
                a[i], b[order - i], (dims, ((), ())), preferred_element_type=jnp.float32
            )
            total = term if total is None else total + term
            yield
    return total


def product(a, b, dims):
    steps = product_steps(a, b, dims)
    while True:
        try:
            next(steps)
        except StopIteration as end:
            return end.value


def ahead_steps(states, known, fixed, found):
    for t, x, along in states:
        if along is not None:
            x = x - (yield from product_steps(along, known[t], NN))
        far = yield from product_steps(parts(x, AHEAD), fixed, NN)
        found.append(parts(jnp.concatenate([x, far], 1), TURN))


NN = ((1,), (0,))
NT = ((1,), (1,))
TN = ((0,), (0,))


def eigen_kernel(lead_ref, cross_ref, trail_ref, rotation_ref, gram_ref, g, turns, z):
    cross = cross_ref[...]
    g[:BLK, :BLK] = lead_ref[...]
    g[:BLK, BLK:] = cross
    g[BLK:, :BLK] = cross.T
    g[BLK:, BLK:] = trail_ref[...]
    panels = 2 * BLK // PANEL
    fixed = parts(g[...], AHEAD)
    ready = {(0, j): g[PANEL * j : PANEL * j + PANEL, :] for j in range(panels)}
    known = {t: None for t in range(ITERS)}
    for stage in range(panels + ITERS - 1):
        active = [(t, stage - t) for t in range(ITERS) if 0 <= stage - t < panels]
        squares, states = [], []
        for t, j in active:
            x = ready.pop((t, j))
            split = parts(x, SQUARE)
            square = product(split, split, NT)
            along = None
            if j > 0:
                along = parts(product(split, known[t], NT), SQUARE)
                square = square - product(along, along, NT)
            squares.append(square)
            states.append((t, x, along))
        found = []
        factors = inverse_factors(squares, WIDE, ahead_steps(states, known, fixed, found))
        for (t, j), both, w in zip(active, found, factors):
            both = product(parts(w, TURN), both, NN)
            turn, ahead = both[:, : 2 * BLK], both[:, 2 * BLK :]
            turns[t, PANEL * j : PANEL * j + PANEL, :] = turn
            if j + 1 < panels:
                split = parts(turn, SQUARE)
                old = known[t]
                known[t] = split if old is None else [
                    jnp.concatenate([a, b], 0) for a, b in zip(old, split)
                ]
            if t + 1 < ITERS:
                ready[t + 1, j] = ahead
            else:
                z[PANEL * j : PANEL * j + PANEL, :] = ahead
    turned = turns[ITERS - 1]
    final = product(parts(turned, AHEAD), parts(z[...], AHEAD), NT)
    rotation_ref[...] = turned.T
    gram_ref[...] = 0.5 * (final + final.T)


def eigen_steps(lead, cross, trail):
    full = jax.ShapeDtypeStruct((2 * BLK, 2 * BLK), jnp.float32)
    vmem = pl.BlockSpec(memory_space=pltpu.VMEM)
    return pl.pallas_call(
        eigen_kernel,
        out_shape=(full, full),
        in_specs=[vmem] * 3,
        out_specs=(vmem, vmem),
        scratch_shapes=[
            pltpu.VMEM((2 * BLK, 2 * BLK), jnp.float32),
            pltpu.VMEM((ITERS, 2 * BLK, 2 * BLK), jnp.float32),
            pltpu.VMEM((2 * BLK, 2 * BLK), jnp.float32),
        ],
        compiler_params=pltpu.CompilerParams(vmem_limit_bytes=32 * 1024 * 1024),
        name="eigen_steps",
    )(lead, cross, trail)


def swapped(x, bit):
    return lax.ppermute(x, "rows", [(i, i ^ bit) for i in range(lax.axis_size("rows"))])


def summed_over(x, groups):
    copies = jnp.broadcast_to(x[None], (len(groups[0]),) + x.shape)
    got = lax.all_to_all(copies, "rows", 0, 0, axis_index_groups=groups)
    return jnp.sum(got, 0)


def along_x():
    size = lax.axis_size("rows")
    return [[c + (size // 4) * j for j in range(4)] for c in range(size // 4)]


def core_halves(x):
    odd = lax.axis_index("rows") % 2 == 1
    half = x.shape[0] // 2
    keep = jnp.where(odd, x[half:], x[:half])
    give = jnp.where(odd, x[:half], x[half:])
    return keep + swapped(give, 1), odd


def both_halves(part, odd):
    other = swapped(part, 1)
    return jnp.where(odd, jnp.concatenate([other, part], 0), jnp.concatenate([part, other], 0))


def moved(x, distance):
    count = lax.axis_size("pairs")
    return lax.ppermute(
        x, "pairs", [(i - distance, i) for i in range(count) if 0 <= i - distance < count]
    )


def big(a, b, dims):
    return lax.dot_general(
        a, b, (dims, ((), ())), precision=lax.Precision.HIGH, preferred_element_type=jnp.float32
    )


def gram_kernel(columns_ref, gram_ref):
    @pl.when(pl.program_id(0) == 0)
    def _():
        gram_ref[...] = jnp.zeros_like(gram_ref)

    split = parts(columns_ref[...], 2)
    gram_ref[...] += product(split, split, TN)


def local_gram(columns):
    rows, width = columns.shape
    return pl.pallas_call(
        gram_kernel,
        grid=(rows // STEP,),
        out_shape=jax.ShapeDtypeStruct((width, width), jnp.float32),
        in_specs=[pl.BlockSpec((STEP, width), lambda i: (i, 0))],
        out_specs=pl.BlockSpec((width, width), lambda i: (0, 0)),
        compiler_params=pltpu.CompilerParams(vmem_limit_bytes=32 * 1024 * 1024),
        name="local_gram",
    )(columns)


def send_kernel(ends_ref, columns_ref, rotation_ref, gram_ref, ahead_ref, back_ref):
    step = pl.program_id(0)
    steps = pl.num_programs(0)
    first = ends_ref[0] == 1
    to_lead, to_trail = rotation_ref[:, :BLK], rotation_ref[:, BLK:]
    ahead = jnp.where(first, to_trail, to_lead)

    @pl.when(step < steps - 1)
    def _():
        both = parts(jnp.concatenate([ahead, to_trail], 1), 2)
        turned = product(parts(columns_ref[...], 2), both, NN)
        ahead_ref[...] = turned[:, :BLK]
        back_ref[...] = turned[:, BLK:]

    @pl.when(step == steps - 1)
    def _():
        trail_gram = gram_ref[BLK:, BLK:]
        ahead_ref[: 2 * BLK, :] = ahead
        ahead_ref[2 * BLK :, :] = jnp.where(first, trail_gram, gram_ref[:BLK, :BLK])
        back_ref[: 2 * BLK, :] = to_trail
        back_ref[2 * BLK :, :] = trail_gram


def to_send(ends, matrix, rotation, gram, late):
    step = 3 * BLK
    steps = late // step
    payload = jax.ShapeDtypeStruct((late + step, BLK), jnp.float32)
    block = pl.BlockSpec((step, BLK), lambda i: (i, 0))
    whole = pl.BlockSpec((2 * BLK, 2 * BLK), lambda i: (0, 0))
    return pl.pallas_call(
        send_kernel,
        grid=(steps + 1,),
        out_shape=(payload, payload),
        in_specs=[
            pl.BlockSpec(memory_space=pltpu.SMEM),
            pl.BlockSpec((step, 2 * BLK), lambda i: (jnp.minimum(i, steps - 1), 0)),
            whole,
            whole,
        ],
        out_specs=(block, block),
        compiler_params=pltpu.CompilerParams(vmem_limit_bytes=32 * 1024 * 1024),
        name="to_send",
    )(ends, matrix, rotation, gram)


def arrive_kernel(
    ends_ref, own_ref, left_ref, left_turn_ref, from_left_ref, right_ref, right_turn_ref,
    from_right_ref, paired_ref, cross_ref,
):
    step = pl.program_id(0)
    steps = pl.num_programs(0)

    @pl.when(step == 0)
    def _():
        cross_ref[...] = jnp.zeros_like(cross_ref)

    def place(left, right):
        leading = jnp.where(ends_ref[0] == 1, own_ref[...], left)
        trailing = jnp.where(ends_ref[1] == 1, own_ref[...], right)
        paired_ref[:, :BLK] = leading
        paired_ref[:, BLK:] = trailing
        cross_ref[...] += product(parts(leading, 2), parts(trailing, 2), TN)

    @pl.when(step < steps - 1)
    def _():
        place(left_ref[...], right_ref[...])

    @pl.when(step == steps - 1)
    def _():
        place(
            product(parts(from_left_ref[...], 2), parts(left_turn_ref[...], 2), NN),
            product(parts(from_right_ref[...], 2), parts(right_turn_ref[...], 2), NN),
        )


def arrived_pair(ends, own, over_left, from_left, over_right, from_right):
    rows = own.shape[0]
    early = from_left.shape[0]
    steps = rows // early
    turn_at = (rows - early) // (2 * BLK)
    over = pl.BlockSpec((early, BLK), lambda i: (jnp.minimum(i, steps - 2), 0))
    turn = pl.BlockSpec((2 * BLK, BLK), lambda i: (turn_at, 0))
    moved_columns = pl.BlockSpec((early, 2 * BLK), lambda i: (0, 0))
    return pl.pallas_call(
        arrive_kernel,
        grid=(steps,),
        out_shape=(
            jax.ShapeDtypeStruct((rows, 2 * BLK), jnp.float32),
            jax.ShapeDtypeStruct((BLK, BLK), jnp.float32),
        ),
        in_specs=[
            pl.BlockSpec(memory_space=pltpu.SMEM),
            pl.BlockSpec((early, BLK), lambda i: (i, 0)),
            over, turn, moved_columns, over, turn, moved_columns,
        ],
        out_specs=(
            pl.BlockSpec((early, 2 * BLK), lambda i: (i, 0)),
            pl.BlockSpec((BLK, BLK), lambda i: (0, 0)),
        ),
        compiler_params=pltpu.CompilerParams(vmem_limit_bytes=32 * 1024 * 1024),
        name="arrived_pair",
    )(ends, own, over_left, over_left, from_left, over_right, over_right, from_right)


def per_device(matrix):
    seat = lax.axis_index("pairs")
    first = seat == 0
    last = seat == lax.axis_size("pairs") - 1
    ends = jnp.stack([first, last]).astype(jnp.int32)
    rows_all = matrix.shape[0] * lax.axis_size("rows")
    late = matrix.shape[0] - matrix.shape[0] // EARLY

    local = local_gram(matrix)
    packed = jnp.concatenate([local[:BLK, :BLK], local[:BLK, BLK:], local[BLK:, BLK:]], 0)
    part, odd = core_halves(packed)
    part = part + swapped(part, 2)

    part, columns = lax.optimization_barrier((part, matrix[late:]))
    from_left = moved(columns, 1)
    from_right = moved(columns, -1)

    packed = both_halves(summed_over(part, along_x()), odd) / rows_all
    rotation, gram = eigen_steps(packed[:BLK], packed[BLK : 2 * BLK], packed[2 * BLK :])
    rotation, gram, from_left, from_right = lax.optimization_barrier(
        (rotation, gram, from_left, from_right)
    )

    ahead, back = to_send(ends, matrix, rotation, gram, late)
    over_left = moved(ahead, 1)
    over_right = moved(back, -1)
    own = big(matrix, rotation[:, :BLK], ((1,), (0,)))
    columns, cross = arrived_pair(ends, own, over_left, from_left, over_right, from_right)
    lead_gram = gram[:BLK, :BLK]
    at = late + 2 * BLK
    new_lead_gram = jnp.where(first, lead_gram, over_left[at:])
    new_trail_gram = jnp.where(last, lead_gram, over_right[at:])

    cross = summed_over(cross + swapped(cross, 1), along_x())
    cross = (cross + swapped(cross, 2)) / rows_all
    rotation, gram = eigen_steps(new_lead_gram, cross, new_trail_gram)
    return big(columns, rotation, ((1,), (0,))), gram


def solution(mesh):
    return jax.shard_map(
        per_device,
        mesh=mesh,
        in_specs=(P("rows", "pairs"),),
        out_specs=(P("rows", "pairs"), P("pairs", None)),
        check_vma=False,
    )
```
